512 devices in a mesh: dp: 8 (over z_lo), tensor: 64 (over x, y, z_hi, core).
Axes of the slice: x: 4, y: 4, z: 16 (z_hi: 2, z_lo: 8; z = z_hi * 8 + z_lo), core: 2. Of those that a mesh axis runs over, the one named last changes fastest.
Arguments:
- attn: bfloat16 [4096, 16384], P('dp', 'tensor'), may hold values from -0.25 to 0.25
- grad_out: bfloat16 [4096, 7168], P(('dp', 'tensor')), may hold values from -24 to 24
- weight: bfloat16 [16384, 7168], P('tensor'), may hold values from -0.0625 to 0.0625
Outputs:
- grad_in: bfloat16 [4096, 16384], P('dp', 'tensor')
- grad_weight: bfloat16 [16384, 7168], P('tensor', 'dp')
The draws below stay inside these ranges and needn't reach their ends.
All inputs are finite; a program needn't handle non-finite values.
Results may differ from the reference program's by a relative error of at most 0.017.
Values may be sent and summed in bfloat16 or wider, within the bound.
No kernel may reach another device: no remote copies, remote signals or barrier semaphores. Data moves between devices by JAX's collectives and lax.ppermute only.
A program may use at most 64 MiB of HBM per device.

```python
import jax
import jax.numpy as jnp
from jax import lax

D = 7168
ROWS = 16384
TOKENS_DP = 512
TOKENS = 4096
N_DP = 8


def strengthened(values, own_key, source, target, blocks, factor):
    def block_of(axis_at):
        return (jnp.arange(values.shape[axis_at]) // (values.shape[axis_at] // blocks)).reshape((-1,) + (1,) * (values.ndim - 1 - axis_at))

    near = jax.random.permutation(own_key, blocks)[block_of(target)]
    far = (block_of(target) + blocks // 2) % blocks
    return jnp.where((block_of(source) == near) | (block_of(source) == far), factor * values, values)


def levels(rng, extent, shards, low, top_value):
    factor_of = 1.0
    for position, shards_of in shards:
        draws = jax.random.uniform(jax.random.fold_in(jax.random.fold_in(rng, 6), position), (shards_of,), jnp.float32, low / len(shards), top_value / len(shards))
        factor_of = factor_of * jnp.repeat(jnp.exp(draws), extent[position] // shards_of).reshape((-1,) + (1,) * (len(extent) - 1 - position))
    return factor_of


def gaussian(key, extent, spread, bound, cuts=(), dtype=jnp.bfloat16):
    drawn = spread * jax.random.normal(key, extent, jnp.float32)
    if cuts:
        drawn = drawn * levels(key, extent, cuts, -0.22, 0.18)
    return jnp.clip(drawn, -bound, bound).astype(dtype)


def bell_draw_with(stream_key, shape, spread, bound, split, heavy, dtype=jnp.bfloat16):
    drawn = spread * jax.random.normal(stream_key, shape, jnp.float32)
    if split:
        drawn = drawn * levels(stream_key, shape, split, -0.22, 0.18)
    return jnp.clip(strengthened(drawn, jax.random.fold_in(stream_key, 3), *heavy), -bound, bound).astype(dtype)


def setup_inputs(seed: int = 0) -> dict:
    seeds = jax.random.split(jax.random.key(seed), 4)
    attn = gaussian(seeds[0], (TOKENS, ROWS), (TOKENS ** -0.5), 0.25, ((0, 8), (1, 64)))
    grad_out = bell_draw_with(seeds[1], (TOKENS, D), 1.0, 24.0, ((0, 512),), (0, 1, 512, 6.0))
    weight = gaussian(seeds[2], (ROWS, D), D ** -0.5, 0.0625, ((0, 64),))
    return {"attn": attn, "grad_out": grad_out, "weight": weight}


def reference(attn, grad_out, weight):
    grad_in = lax.dot_general(grad_out, weight, (((1,), (1,)), ((), ())), preferred_element_type=jnp.float32).astype(jnp.bfloat16)
    groups_attn = attn.reshape(N_DP, TOKENS_DP, ROWS)
    groups_grad = grad_out.reshape(N_DP, TOKENS_DP, D)

    def accumulate(total, pair):
        part = lax.dot_general(pair[0], pair[1], (((0,), (0,)), ((), ())), preferred_element_type=jnp.float32)
        rounded = lax.optimization_barrier(part.astype(jnp.bfloat16))
        return total + rounded.astype(jnp.float32), None

    start = jnp.zeros((ROWS, D), jnp.float32)
    total, unused = lax.scan(accumulate, start, (groups_attn, groups_grad))
    return grad_in, total.astype(jnp.bfloat16)
```

```python
import jax
import jax.numpy as jnp
from jax import lax
from jax.sharding import Mesh, PartitionSpec as P

NX, NY, NZ, NC = 4, 4, 2, 2
AXES = ("dp", "x", "y", "zh", "core")


def contract_tokens(left, right):
    return lax.dot_general(
        left, right, (((0,), (0,)), ((), ())), preferred_element_type=jnp.float32
    )


def contract_width(left, right):
    return lax.dot_general(
        left, right, (((1,), (1,)), ((), ())), preferred_element_type=jnp.float32
    )


def shift(values, step, first):
    pairs = []
    for x in range(NX):
        for y in range(NY):
            for c in range(NC):
                if (c == 0) == first:
                    to = ((x + step) % NX, y)
                else:
                    to = (x, (y + step) % NY)
                pairs.append(((x * NY + y) * NC + c, (to[0] * NY + to[1]) * NC + c))
    return lax.ppermute(values, ("x", "y", "core"), pairs)


def swap(values, axis):
    return lax.ppermute(values, axis, [(0, 1), (1, 0)])


def stage(values, first):
    plus = shift(values, 1, first)
    minus = shift(values, -1, first)
    far = shift(values, 2, first)
    return [values, plus, far, minus]


def relative(values, axis, at):
    n = values.shape[axis]
    turned = lax.rev(values, (axis,))
    doubled = jnp.concatenate([turned, turned], axis)
    return lax.dynamic_slice_in_dim(doubled, n - 1 - at, n, axis)


def body(attn, grad_out, weight):
    x, y, z, c = (lax.axis_index(a) for a in ("x", "y", "zh", "core"))
    n_dp = lax.axis_size("dp")
    rows = attn.shape[1]
    held = grad_out.shape[0]
    width = grad_out.shape[1]
    columns = width // n_dp

    both = jnp.concatenate([grad_out, swap(grad_out, "zh")], 0)
    sliced = lax.all_to_all(both, "dp", 1, 0, tiled=True)

    by_core = attn.reshape(NX * NY * NZ, NC, held, rows)
    mine = lax.dynamic_index_in_dim(by_core, c, 1, keepdims=False)
    other = lax.dynamic_index_in_dim(by_core, 1 - c, 1, keepdims=False)
    wide = jnp.concatenate([mine, swap(other, "core")], -1)
    wide = wide.reshape(NX, NY, NZ, held, NC * rows)
    wide = jnp.where(z == 0, wide, wide[:, :, ::-1])
    wide = jnp.where(c == 0, wide.swapaxes(0, 1), wide)
    wide = relative(relative(wide, 0, jnp.where(c == 0, y, x)), 1, jnp.where(c == 0, x, y))
    tokens = NX * NY * NZ * held
    gathered = lax.all_gather(wide.reshape(tokens, NC * rows), "dp", axis=0, tiled=True)
    gathered = gathered.reshape(n_dp, NX * NY, NZ * held, NC * rows)
    gathered = gathered.swapaxes(0, 1).reshape(NX, NY * n_dp * NZ * held, NC * rows)

    weight_other = swap(weight, "core")

    line = jnp.concatenate(stage(both, True), 0)
    group = jnp.concatenate(stage(line, False), 0)
    near = contract_width(group, weight).astype(jnp.bfloat16)
    far = contract_width(group, weight_other).astype(jnp.bfloat16)
    far = swap(far, "core")

    def placed(part, core):
        part = part.reshape(NX, NY, NZ, held, rows)
        part = relative(relative(part, 0, jnp.where(core == 0, y, x)), 1, jnp.where(core == 0, x, y))
        part = jnp.where(core == 0, part.swapaxes(0, 1), part)
        return jnp.where(z == 0, part, part[:, :, ::-1])

    near, far = placed(near, c), placed(far, 1 - c)
    low, high = jnp.where(c == 0, near, far), jnp.where(c == 0, far, near)
    grad_in = jnp.stack([low, high], 3).reshape(NX * NY * NZ * NC * held, rows)

    strip = jnp.concatenate(stage(sliced, True), 0)
    total = jnp.zeros((NC * rows, columns), jnp.float32)
    for part, piece in zip(gathered, stage(strip, False)):
        total = total + contract_tokens(part, piece)
    grad_weight = (total[:rows] + swap(total[rows:], "core")).astype(jnp.bfloat16)
    return grad_in, grad_weight


def solution(mesh):
    n_dp = mesh.shape["dp"]
    fine = Mesh(mesh.devices.reshape(n_dp, NX, NY, NZ, NC), AXES)
    tensor = ("x", "y", "zh", "core")
    in_specs = (P("dp", tensor), P(("dp",) + tensor, None), P(tensor, None))
    out_specs = (P("dp", tensor), P(tensor, "dp"))
    return jax.shard_map(body, mesh=fine, in_specs=in_specs, out_specs=out_specs, check_vma=False)
```

```python
import functools

import jax
import jax.numpy as jnp
from jax import lax
from jax.experimental import pallas as pl
from jax.experimental.pallas import tpu as pltpu
from jax.sharding import Mesh, PartitionSpec as P

NX, NY, NZ, NC = 4, 4, 2, 2
AXES = ("dp", "x", "y", "zh", "core")
RING = (0, 2, 4, 6, 7, 5, 3, 1)
BEFORE = tuple(RING[(RING.index(g) - k) % len(RING)] for g in range(len(RING)) for k in range(len(RING)))
TENSOR = ("x", "y", "zh", "core")


def lines(first):
    def at(x, y, z, c):
        return ((x * NY + y) * NZ + z) * NC + c

    groups = []
    for z in range(NZ):
        for c in range(NC):
            for k in range(NX):
                if (c == 0) == first:
                    groups.append([at(i, k, z, c) for i in range(NX)])
                else:
                    groups.append([at(k, i, z, c) for i in range(NY)])
    return groups


def spread(values, first):
    n = values.shape[0]
    copies = jnp.broadcast_to(values[None], (NX,) + values.shape).reshape((NX * n,) + values.shape[1:])
    return lax.all_to_all(copies, TENSOR, 0, 0, axis_index_groups=lines(first), tiled=True)


def turn(values, step):
    pairs = [(RING[i], RING[(i + step) % len(RING)]) for i in range(len(RING))]
    return lax.ppermute(values, "dp", pairs)


def swap(values, axis):
    return lax.ppermute(values, axis, [(0, 1), (1, 0)])


def place_kernel(place, near, far, out):
    zh, c = place[2], place[3]
    for part, core in ((near, c), (far, 1 - c)):
        for at in range(near.shape[0]):
            at2, at1, turned = at // (NX * NZ), (at // NZ) % NX, at % NZ
            px, py = jnp.where(core == 0, at1, at2), jnp.where(core == 0, at2, at1)
            z = zh if turned == 0 else 1 - zh
            out[((px * NY + py) * NZ + z) * NC + core] = part[at]


def small(kernel, shape, place, *values):
    return pl.pallas_call(
        kernel,
        out_shape=jax.ShapeDtypeStruct(shape, values[0].dtype),
        in_specs=[pl.BlockSpec(memory_space=pltpu.SMEM)]
        + [pl.BlockSpec(memory_space=pltpu.VMEM)] * len(values),
        out_specs=pl.BlockSpec(memory_space=pltpu.VMEM),
    )(place, *values)


def width_kernel(moved, mine, theirs, near, far, total):
    at = pl.program_id(0)
    chips, _, parts, _, columns = moved.shape
    left = jnp.concatenate(
        [jnp.concatenate([moved[i, 0, j] for i in range(chips)], 0) for j in range(parts)], 1
    )
    for step in range(2):
        @pl.when(at == step)
        def _(step=step):
            for half, (right, out) in enumerate(((theirs, far), (mine, near))):
                term = lax.dot_general(
                    left, right[:, step * parts * columns:(step + 1) * parts * columns],
                    (((1,), (1,)), ((), ())), preferred_element_type=jnp.float32,
                )
                if step == 0:
                    total[half] = term
                else:
                    out[...] = (total[half] + term).astype(out.dtype)


def contract_width(moved, weight, weight_other):
    chips, _, parts, deep, columns = moved.shape
    rows = weight.shape[0]
    tokens = chips * deep
    shape = jax.ShapeDtypeStruct((tokens, rows), weight.dtype)
    whole = pl.BlockSpec((tokens, rows), lambda i: (0, 0))
    return pl.pallas_call(
        width_kernel,
        grid=(2,),
        out_shape=(shape, shape),
        in_specs=[
            pl.BlockSpec((chips, 1, parts // 2, deep, columns), lambda i: (0, 0, i, 0, 0)),
            pl.BlockSpec(memory_space=pltpu.VMEM), pl.BlockSpec(memory_space=pltpu.VMEM),
        ],
        out_specs=(whole, whole),
        scratch_shapes=[pltpu.VMEM((2, tokens, rows), jnp.float32)],
        compiler_params=pltpu.CompilerParams(vmem_limit_bytes=24 * 1024 * 1024),
        cost_estimate=pl.CostEstimate(
            flops=4 * tokens * rows * parts * columns, bytes_accessed=11 * 1024 * 1024, transcendentals=0
        ),
    )(moved, weight, weight_other)


def tokens_kernel(ring, *refs):
    blocks, parts, near, far, total = refs[:4], refs[4:-3], refs[-3], refs[-2], refs[-1]
    at = pl.program_id(0)
    right = jnp.concatenate([block[i, 0, 0] for block in blocks for i in range(block.shape[0])], 0)
    for step in range(len(parts) // 4):
        @pl.when(at == step)
        def _(step=step):
            left = jnp.concatenate([part[...] for part in parts[4 * step:4 * step + 4]], 1)
            term = jnp.dot(left, right, preferred_element_type=jnp.float32)
            if step == 0:
                total[...] = term
            else:
                rows = near.shape[0]
                near[...] = total[:rows] + term[:rows]
                far[...] = (total[rows:] + term[rows:]).astype(far.dtype)


def contract_tokens(ring, moved, parts):
    chips, _, n_dp, deep, columns = moved.shape
    rows, tokens = parts[0].shape
    half = rows // NC
    whole = pl.BlockSpec((half, columns), lambda k, ring: (0, 0))
    shape = (chips, 1, 1, deep, columns)
    return pl.pallas_call(
        tokens_kernel,
        out_shape=(
            jax.ShapeDtypeStruct((half, columns), jnp.float32), jax.ShapeDtypeStruct((half, columns), jnp.bfloat16)
        ),
        grid_spec=pltpu.PrefetchScalarGridSpec(
            num_scalar_prefetch=1,
            grid=(n_dp // 4,),
            in_specs=[
                pl.BlockSpec(shape, lambda k, ring, j=j: (0, 1, ring[4 * k + j], 0, 0)) for j in range(4)
            ] + [pl.BlockSpec(memory_space=pltpu.VMEM)] * n_dp,
            out_specs=(whole, whole),
            scratch_shapes=[pltpu.VMEM((rows, columns), jnp.float32)],
        ),
        compiler_params=pltpu.CompilerParams(vmem_limit_bytes=24 * 1024 * 1024),
        cost_estimate=pl.CostEstimate(
            flops=2 * rows * tokens * n_dp * columns, bytes_accessed=8 * 1024 * 1024, transcendentals=0
        ),
    )(ring, *[moved] * 4, *parts)


def body(attn, grad_out, weight):
    place = jnp.stack([lax.axis_index(a) for a in TENSOR + ("dp",)]).astype(jnp.int32)
    c = place[3]
    n_dp = lax.axis_size("dp")
    rows = attn.shape[1]
    held, width = grad_out.shape
    columns = width // n_dp
    blocks = NX * NY * NZ
    tokens = blocks * held
    deep = NZ * held

    parts = attn.reshape(NX, NY, NZ, NC, held, rows)
    low, high = parts[:, :, :, 0].swapaxes(0, 1), parts[:, :, :, 1]
    mine = jnp.where(c == 0, low, high).reshape(tokens, rows).T
    other = jnp.where(c == 0, high, low).reshape(tokens, rows).T
    wide = jnp.concatenate([mine, swap(other, "core")], 0)

    strips = jnp.broadcast_to(
        grad_out.reshape(held, n_dp, 1, columns).transpose(1, 2, 0, 3), (n_dp, NZ, held, columns)
    ).reshape(n_dp * deep, columns)
    sliced = lax.all_to_all(strips, ("dp", "zh"), 0, 0, tiled=True)
    both = jnp.concatenate([grad_out, swap(grad_out, "zh")], 0)
    both = both.reshape(deep, n_dp, columns).swapaxes(0, 1).reshape(n_dp * deep, columns)

    both, wide = lax.optimization_barrier((both, wide))
    moved = spread(jnp.concatenate([both, sliced], 0), True)
    weight_other = swap(weight, "core")

    wide, _ = lax.optimization_barrier((wide, sliced))
    ahead, back = [wide, turn(wide, 1)], [wide, turn(wide, -1)]
    moved, ahead[1], back[1] = lax.optimization_barrier((moved, ahead[1], back[1]))
    moved = spread(moved, False).reshape(NX * NY, 2, n_dp, deep, columns)
    for _ in range(n_dp // 2 - 1):
        ahead.append(turn(ahead[-1], 1))
    for _ in range(n_dp // 2 - 2):
        back.append(turn(back[-1], -1))
    ring = lax.dynamic_slice_in_dim(jnp.asarray(BEFORE, jnp.int32), place[4] * n_dp, n_dp)

    total, part = contract_tokens(ring, moved, ahead + back[:0:-1])
    part = swap(part, "core")
    near, far = contract_width(moved, weight, weight_other)
    far = swap(far, "core")
    grad_weight = (total + part.astype(jnp.float32)).astype(jnp.bfloat16)
    grad_in = small(
        place_kernel, (NC * blocks, held, rows), place, near.reshape(blocks, held, rows), far.reshape(blocks, held, rows)
    ).reshape(NC * tokens, rows)
    return grad_in, grad_weight


def solution(mesh):
    n_dp = mesh.shape["dp"]
    fine = Mesh(mesh.devices.reshape(n_dp, NX, NY, NZ, NC), AXES)
    in_specs = (P("dp", TENSOR), P(("dp",) + TENSOR, None), P(TENSOR, None))
    out_specs = (P("dp", TENSOR), P(TENSOR, "dp"))
    return jax.shard_map(body, mesh=fine, in_specs=in_specs, out_specs=out_specs, check_vma=False)
```

```python
import functools

import jax
import jax.numpy as jnp
from jax import lax
from jax.experimental import pallas as pl
from jax.experimental.pallas import tpu as pltpu
from jax.sharding import Mesh, PartitionSpec as P

NX, NY, NZ, NC = 4, 4, 2, 2
AXES = ("dp", "x", "y", "zh", "core")
RING = (0, 2, 4, 6, 7, 5, 3, 1)
BEFORE = tuple(RING[(RING.index(g) - k) % len(RING)] for g in range(len(RING)) for k in range(len(RING)))
TENSOR = ("x", "y", "zh", "core")


def lines(first):
    def at(x, y, z, c):
        return ((x * NY + y) * NZ + z) * NC + c

    groups = []
    for z in range(NZ):
        for c in range(NC):
            for k in range(NX):
                if (c == 0) == first:
                    groups.append([at(i, k, z, c) for i in range(NX)])
                else:
                    groups.append([at(k, i, z, c) for i in range(NY)])
    return groups


def spread(values, first):
    n = values.shape[0]
    copies = jnp.broadcast_to(values[None], (NX,) + values.shape).reshape((NX * n,) + values.shape[1:])
    return lax.all_to_all(copies, TENSOR, 0, 0, axis_index_groups=lines(first), tiled=True)


def turn(values, step):
    pairs = [(RING[i], RING[(i + step) % len(RING)]) for i in range(len(RING))]
    return lax.ppermute(values, "dp", pairs)


def swap(values, axis):
    return lax.ppermute(values, axis, [(0, 1), (1, 0)])


def products_kernel(ring, moved, mine, theirs, *refs):
    parts, refs = refs[:-8], refs[-8:]
    near_in, near_weight, far, wide, strips, weights, total, sems = refs
    chips, _, n_dp, _, columns = moved.shape
    rows = near_weight.shape[0]
    half = n_dp // 2
    blocks = far.shape[0]

    arrive = [
        pltpu.make_async_copy(moved.at[:, 1, ring[k]], strips.at[k], sems.at[k]) for k in range(n_dp)
    ]
    for copy in arrive:
        copy.start()
    fetch = []
    for h in range(2):
        cut = pl.ds(h * half * columns, half * columns)
        at = n_dp + 3 * h
        fetch.append([
            pltpu.make_async_copy(moved.at[:, 0, pl.ds(h * half, half)], wide.at[h], sems.at[at]),
            pltpu.make_async_copy(mine.at[:, cut], weights.at[0, h], sems.at[at + 1]),
            pltpu.make_async_copy(theirs.at[:, cut], weights.at[1, h], sems.at[at + 2]),
        ])
        for copy in fetch[h]:
            copy.start()

    for h in range(2):
        for copy in arrive[h * half:(h + 1) * half]:
            copy.wait()
        right = jnp.concatenate(
            [strips[k, i] for k in range(h * half, (h + 1) * half) for i in range(chips)], 0
        )
        left = jnp.concatenate([part[...] for part in parts[h * half:(h + 1) * half]], 1)
        term = jnp.dot(left, right, preferred_element_type=jnp.float32)
        if h == 0:
            total[...] = term
        else:
            near_weight[...] = total[:rows] + term[:rows]
            part = total[rows:] + term[rows:]
            far[:, :, rows:] = part.reshape(blocks, -1, columns).astype(far.dtype)

    sums = [None, None]
    for h in range(2):
        for copy in fetch[h]:
            copy.wait()
        left = jnp.concatenate(
            [jnp.concatenate([wide[h, i, j] for i in range(chips)], 0) for j in range(half)], 1
        )
        for at in range(NC):
            term = lax.dot_general(
                left, weights[at, h], (((1,), (1,)), ((), ())), preferred_element_type=jnp.float32
            )
            sums[at] = term if h == 0 else sums[at] + term
    near_in[...] = sums[0].reshape(blocks, -1, rows).astype(near_in.dtype)
    far[:, :, :rows] = sums[1].reshape(blocks, -1, rows).astype(far.dtype)


def products(ring, moved, weight, weight_other, parts, held):
    chips, _, n_dp, deep, columns = moved.shape
    rows = weight.shape[0]
    blocks = chips * deep // held
    vmem, whole = pl.BlockSpec(memory_space=pltpu.VMEM), pl.BlockSpec(memory_space=pl.ANY)
    return pl.pallas_call(
        products_kernel,
        out_shape=(
            jax.ShapeDtypeStruct((blocks, held, rows), jnp.bfloat16),
            jax.ShapeDtypeStruct((rows, columns), jnp.float32),
            jax.ShapeDtypeStruct((blocks, held, rows + columns), jnp.bfloat16),
        ),
        in_specs=[pl.BlockSpec(memory_space=pltpu.SMEM), whole, pl.BlockSpec(memory_space=pltpu.HBM), whole]
        + [vmem] * len(parts),
        out_specs=(vmem, vmem, vmem),
        scratch_shapes=[
            pltpu.VMEM((2, chips, n_dp // 2, deep, columns), jnp.bfloat16),
            pltpu.VMEM((n_dp, chips, deep, columns), jnp.bfloat16),
            pltpu.VMEM((NC, 2, rows, n_dp // 2 * columns), jnp.bfloat16),
            pltpu.VMEM((NC * rows, columns), jnp.float32),
            pltpu.SemaphoreType.DMA((n_dp + 6,)),
        ],
        compiler_params=pltpu.CompilerParams(vmem_limit_bytes=50 * 1024 * 1024),
        cost_estimate=pl.CostEstimate(
            flops=8 * blocks * held * rows * n_dp * columns, bytes_accessed=17 * 1024 * 1024, transcendentals=0
        ),
    )(ring, moved, weight, weight_other, *parts)


def finish_kernel(place, near_in, near_weight, far, grad_in, grad_weight):
    zh, c = place[2], place[3]
    rows = near_in.shape[-1]
    for part, core in ((near_in, c), (far, 1 - c)):
        for at in range(near_in.shape[0]):
            at2, at1, turned = at // (NX * NZ), (at // NZ) % NX, at % NZ
            px, py = jnp.where(core == 0, at1, at2), jnp.where(core == 0, at2, at1)
            z = zh if turned == 0 else 1 - zh
            grad_in[((px * NY + py) * NZ + z) * NC + core] = part[at, :, :rows]
    part = far[:, :, rows:].astype(jnp.float32).reshape(near_weight.shape)
    grad_weight[...] = (near_weight[...] + part).astype(grad_weight.dtype)


def finish(place, near_in, near_weight, far):
    blocks, held, rows = near_in.shape
    vmem = pl.BlockSpec(memory_space=pltpu.VMEM)
    return pl.pallas_call(
        finish_kernel,
        out_shape=(
            jax.ShapeDtypeStruct((NC * blocks, held, rows), jnp.bfloat16),
            jax.ShapeDtypeStruct(near_weight.shape, jnp.bfloat16),
        ),
        in_specs=[pl.BlockSpec(memory_space=pltpu.SMEM), vmem, vmem, vmem],
        out_specs=(vmem, vmem),
        compiler_params=pltpu.CompilerParams(vmem_limit_bytes=8 * 1024 * 1024),
    )(place, near_in, near_weight, far)


def body(attn, grad_out, weight):
    place = jnp.stack([lax.axis_index(a) for a in TENSOR + ("dp",)]).astype(jnp.int32)
    c = place[3]
    n_dp = lax.axis_size("dp")
    rows = attn.shape[1]
    held, width = grad_out.shape
    columns = width // n_dp
    blocks = NX * NY * NZ
    tokens = blocks * held
    deep = NZ * held

    parts = attn.reshape(NX, NY, NZ, NC, held, rows)
    low, high = parts[:, :, :, 0].swapaxes(0, 1), parts[:, :, :, 1]
    mine = jnp.where(c == 0, low, high).reshape(tokens, rows).T
    other = jnp.where(c == 0, high, low).reshape(tokens, rows).T
    wide = jnp.concatenate([mine, swap(other, "core")], 0)

    strips = jnp.broadcast_to(
        grad_out.reshape(held, n_dp, 1, columns).transpose(1, 2, 0, 3), (n_dp, NZ, held, columns)
    ).reshape(n_dp * deep, columns)
    sliced = lax.all_to_all(strips, ("dp", "zh"), 0, 0, tiled=True)
    both = jnp.concatenate([grad_out, swap(grad_out, "zh")], 0)
    both = both.reshape(deep, n_dp, columns).swapaxes(0, 1).reshape(n_dp * deep, columns)

    both, wide = lax.optimization_barrier((both, wide))
    moved = spread(jnp.concatenate([both, sliced], 0), True)
    weight_other = swap(weight, "core")

    wide, _ = lax.optimization_barrier((wide, sliced))
    ahead, back = [wide, turn(wide, 1)], [wide, turn(wide, -1)]
    moved, ahead[1], back[1] = lax.optimization_barrier((moved, ahead[1], back[1]))
    moved = spread(moved, False).reshape(NX * NY, 2, n_dp, deep, columns)
    for _ in range(n_dp // 2 - 1):
        ahead.append(turn(ahead[-1], 1))
    for _ in range(n_dp // 2 - 2):
        back.append(turn(back[-1], -1))
    ring = lax.dynamic_slice_in_dim(jnp.asarray(BEFORE, jnp.int32), place[4] * n_dp, n_dp)

    near_in, near_weight, far = products(ring, moved, weight, weight_other, ahead + back[:0:-1], held)
    far = swap(far, "core")
    grad_in, grad_weight = finish(place, near_in, near_weight, far)
    return grad_in.reshape(NC * tokens, rows), grad_weight


def solution(mesh):
    n_dp = mesh.shape["dp"]
    fine = Mesh(mesh.devices.reshape(n_dp, NX, NY, NZ, NC), AXES)
    in_specs = (P("dp", TENSOR), P(("dp",) + TENSOR, None), P(TENSOR, None))
    out_specs = (P("dp", TENSOR), P(TENSOR, "dp"))
    return jax.shard_map(body, mesh=fine, in_specs=in_specs, out_specs=out_specs, check_vma=False)
```

```python
import functools

import jax
import jax.numpy as jnp
from jax import lax
from jax.experimental import pallas as pl
from jax.experimental.pallas import tpu as pltpu
from jax.sharding import Mesh, PartitionSpec as P

NX, NY, NZ, NC = 4, 4, 2, 2
AXES = ("dp", "x", "y", "zh", "core")
RING = (0, 2, 4, 6, 7, 5, 3, 1)
LAST = len(RING) - 1


def place_of(g, other):
    return g if other == g else len(RING) + (g if other == LAST else other)


BEFORE = tuple(
    place_of(g, RING[(RING.index(g) - k) % len(RING)]) for g in range(len(RING)) for k in range(len(RING))
)
TENSOR = ("x", "y", "zh", "core")


def lines(first):
    def at(x, y, z, c):
        return ((x * NY + y) * NZ + z) * NC + c

    groups = []
    for z in range(NZ):
        for c in range(NC):
            for k in range(NX):
                if (c == 0) == first:
                    groups.append([at(i, k, z, c) for i in range(NX)])
                else:
                    groups.append([at(k, i, z, c) for i in range(NY)])
    return groups


def spread(values, first):
    n = values.shape[0]
    copies = jnp.broadcast_to(values[None], (NX,) + values.shape).reshape((NX * n,) + values.shape[1:])
    return lax.all_to_all(copies, TENSOR, 0, 0, axis_index_groups=lines(first), tiled=True)


def turn(values, step):
    pairs = [(RING[i], RING[(i + step) % len(RING)]) for i in range(len(RING))]
    return lax.ppermute(values, "dp", pairs)


def swap(values, axis):
    return lax.ppermute(values, axis, [(0, 1), (1, 0)])


def products_kernel(ring, moved, mine, theirs, *refs):
    parts, refs = refs[:-8], refs[-8:]
    near_in, near_weight, far, wide, strips, weights, total, sems = refs
    chips, _, _, columns = moved.shape
    n_dp, rows = len(parts), near_weight.shape[0]
    half = n_dp // 2
    blocks = far.shape[0]

    arrive = [
        pltpu.make_async_copy(moved.at[:, ring[k]], strips.at[k], sems.at[k]) for k in range(n_dp)
    ]
    for copy in arrive:
        copy.start()
    fetch = []
    for h in range(2):
        cut = pl.ds(h * half * columns, half * columns)
        at = n_dp + 3 * h
        fetch.append([
            pltpu.make_async_copy(moved.at[:, pl.ds(h * half, half)], wide.at[h], sems.at[at]),
            pltpu.make_async_copy(mine.at[:, cut], weights.at[0, h], sems.at[at + 1]),
            pltpu.make_async_copy(theirs.at[:, cut], weights.at[1, h], sems.at[at + 2]),
        ])
        for copy in fetch[h]:
            copy.start()

    for h in range(2):
        for copy in arrive[h * half:(h + 1) * half]:
            copy.wait()
        right = jnp.concatenate(
            [strips[k, i] for k in range(h * half, (h + 1) * half) for i in range(chips)], 0
        )
        left = jnp.concatenate([part[...] for part in parts[h * half:(h + 1) * half]], 1)
        term = jnp.dot(left, right, preferred_element_type=jnp.float32)
        if h == 0:
            total[...] = term
        else:
            near_weight[...] = total[:rows] + term[:rows]
            part = total[rows:] + term[rows:]
            far[:, :, rows:] = part.reshape(blocks, -1, columns).astype(far.dtype)

    sums = [None, None]
    for h in range(2):
        for copy in fetch[h]:
            copy.wait()
        left = jnp.concatenate(
            [jnp.concatenate([wide[h, i, j] for i in range(chips)], 0) for j in range(half)], 1
        )
        for at in range(NC):
            term = lax.dot_general(
                left, weights[at, h], (((1,), (1,)), ((), ())), preferred_element_type=jnp.float32
            )
            sums[at] = term if h == 0 else sums[at] + term
    near_in[...] = sums[0].reshape(blocks, -1, rows).astype(near_in.dtype)
    far[:, :, :rows] = sums[1].reshape(blocks, -1, rows).astype(far.dtype)


def products(ring, moved, weight, weight_other, parts, held):
    chips, _, deep, columns = moved.shape
    n_dp, rows = len(parts), weight.shape[0]
    blocks = chips * deep // held
    vmem, whole = pl.BlockSpec(memory_space=pltpu.VMEM), pl.BlockSpec(memory_space=pl.ANY)
    return pl.pallas_call(
        products_kernel,
        out_shape=(
            jax.ShapeDtypeStruct((blocks, held, rows), jnp.bfloat16),
            jax.ShapeDtypeStruct((rows, columns), jnp.float32),
            jax.ShapeDtypeStruct((blocks, held, rows + columns), jnp.bfloat16),
        ),
        in_specs=[pl.BlockSpec(memory_space=pltpu.SMEM), whole, pl.BlockSpec(memory_space=pltpu.HBM), whole]
        + [vmem] * len(parts),
        out_specs=(vmem, vmem, vmem),
        scratch_shapes=[
            pltpu.VMEM((2, chips, n_dp // 2, deep, columns), jnp.bfloat16),
            pltpu.VMEM((n_dp, chips, deep, columns), jnp.bfloat16),
            pltpu.VMEM((NC, 2, rows, n_dp // 2 * columns), jnp.bfloat16),
            pltpu.VMEM((NC * rows, columns), jnp.float32),
            pltpu.SemaphoreType.DMA((n_dp + 6,)),
        ],
        compiler_params=pltpu.CompilerParams(vmem_limit_bytes=50 * 1024 * 1024),
        cost_estimate=pl.CostEstimate(
            flops=8 * blocks * held * rows * n_dp * columns, bytes_accessed=17 * 1024 * 1024, transcendentals=0
        ),
    )(ring, moved, weight, weight_other, *parts)


def finish_kernel(place, near_in, near_weight, far, grad_in, grad_weight):
    zh, c = place[2], place[3]
    rows = near_in.shape[-1]
    for part, core in ((near_in, c), (far, 1 - c)):
        for at in range(near_in.shape[0]):
            at2, at1, turned = at // (NX * NZ), (at // NZ) % NX, at % NZ
            px, py = jnp.where(core == 0, at1, at2), jnp.where(core == 0, at2, at1)
            z = zh if turned == 0 else 1 - zh
            grad_in[((px * NY + py) * NZ + z) * NC + core] = part[at, :, :rows]
    part = far[:, :, rows:].astype(jnp.float32).reshape(near_weight.shape)
    grad_weight[...] = (near_weight[...] + part).astype(grad_weight.dtype)


def finish(place, near_in, near_weight, far):
    blocks, held, rows = near_in.shape
    vmem = pl.BlockSpec(memory_space=pltpu.VMEM)
    return pl.pallas_call(
        finish_kernel,
        out_shape=(
            jax.ShapeDtypeStruct((NC * blocks, held, rows), jnp.bfloat16),
            jax.ShapeDtypeStruct(near_weight.shape, jnp.bfloat16),
        ),
        in_specs=[pl.BlockSpec(memory_space=pltpu.SMEM), vmem, vmem, vmem],
        out_specs=(vmem, vmem),
        compiler_params=pltpu.CompilerParams(vmem_limit_bytes=8 * 1024 * 1024),
    )(place, near_in, near_weight, far)


def body(attn, grad_out, weight):
    place = jnp.stack([lax.axis_index(a) for a in TENSOR + ("dp",)]).astype(jnp.int32)
    zh, c, dp = place[2], place[3], place[4]
    n_dp = lax.axis_size("dp")
    rows = attn.shape[1]
    held, width = grad_out.shape
    columns = width // n_dp
    blocks = NX * NY * NZ
    tokens = blocks * held
    deep = NZ * held

    parts = attn.reshape(NX, NY, NZ, NC, held, rows)
    low, high = parts[:, :, :, 0].swapaxes(0, 1), parts[:, :, :, 1]
    mine = jnp.where(c == 0, low, high).reshape(tokens, rows).T
    other = jnp.where(c == 0, high, low).reshape(tokens, rows).T
    wide = jnp.concatenate([mine, swap(other, "core")], 0)

    strips = jnp.broadcast_to(
        grad_out.reshape(held, n_dp, 1, columns).transpose(1, 2, 0, 3), (n_dp, NZ, held, columns)
    ).reshape(n_dp * deep, columns)
    sliced = lax.all_to_all(strips, ("dp", "zh"), 0, 0, tiled=True).reshape(n_dp, deep, columns)
    own = lax.broadcasted_iota(jnp.int32, (LAST, 1, 1), 0) == dp
    others = jnp.where(own, sliced[LAST:], sliced[:LAST]).reshape(LAST * deep, columns)
    both = jnp.concatenate([grad_out, swap(grad_out, "zh")], 0)
    both = both.reshape(deep, n_dp, columns).swapaxes(0, 1).reshape(n_dp * deep, columns)

    weight_other = swap(weight, "core")
    wide, both = lax.optimization_barrier((wide, both))
    ahead, back = [wide, turn(wide, 1)], [wide]
    both, ahead[1] = lax.optimization_barrier((both, ahead[1]))
    moved = spread(jnp.concatenate([both, others], 0), True)
    ahead.append(turn(ahead[-1], 1))
    back.append(turn(wide, -1))
    moved, ahead[2], back[1] = lax.optimization_barrier((moved, ahead[2], back[1]))
    moved = spread(moved, False).reshape(NX * NY, n_dp + LAST, deep, columns)
    for _ in range(n_dp // 2 - 2):
        ahead.append(turn(ahead[-1], 1))
        back.append(turn(back[-1], -1))
    ring = lax.dynamic_slice_in_dim(jnp.asarray(BEFORE, jnp.int32), dp * n_dp, n_dp)

    first = wide.reshape(NC * rows, NX * NY, NZ, held)
    first = jnp.where(zh == 0, first, first[:, :, ::-1]).reshape(NC * rows, tokens)
    near_in, near_weight, far = products(ring, moved, weight, weight_other, [first] + ahead[1:] + back[:0:-1], held)
    far = swap(far, "core")
    grad_in, grad_weight = finish(place, near_in, near_weight, far)
    return grad_in.reshape(NC * tokens, rows), grad_weight


def solution(mesh):
    n_dp = mesh.shape["dp"]
    fine = Mesh(mesh.devices.reshape(n_dp, NX, NY, NZ, NC), AXES)
    in_specs = (P("dp", TENSOR), P(("dp",) + TENSOR, None), P(TENSOR, None))
    out_specs = (P("dp", TENSOR), P(TENSOR, "dp"))
    return jax.shard_map(body, mesh=fine, in_specs=in_specs, out_specs=out_specs, check_vma=False)
```

```python
import functools

import jax
import jax.numpy as jnp
from jax import lax
from jax.experimental import pallas as pl
from jax.experimental.pallas import tpu as pltpu
from jax.sharding import Mesh, PartitionSpec as P

NX, NY, NZ, NC = 4, 4, 2, 2
AXES = ("dp", "x", "y", "zh", "core")
RING = (0, 2, 4, 6, 7, 5, 3, 1)
LAST = len(RING) - 1


def place_of(g, other):
    return g if other == g else len(RING) + (g if other == LAST else other)


BEFORE = tuple(
    place_of(g, RING[(RING.index(g) - k) % len(RING)]) for g in range(len(RING)) for k in range(len(RING))
)
TENSOR = ("x", "y", "zh", "core")


def lines(first):
    def at(x, y, z, c):
        return ((x * NY + y) * NZ + z) * NC + c

    groups = []
    for z in range(NZ):
        for c in range(NC):
            for k in range(NX):
                if (c == 0) == first:
                    groups.append([at(i, k, z, c) for i in range(NX)])
                else:
                    groups.append([at(k, i, z, c) for i in range(NY)])
    return groups


def spread(values, first):
    n = values.shape[0]
    copies = jnp.broadcast_to(values[None], (NX,) + values.shape).reshape((NX * n,) + values.shape[1:])
    return lax.all_to_all(copies, TENSOR, 0, 0, axis_index_groups=lines(first), tiled=True)


def turn(values, step):
    pairs = [(RING[i], RING[(i + step) % len(RING)]) for i in range(len(RING))]
    return lax.ppermute(values, "dp", pairs)


def swap(values, axis):
    return lax.ppermute(values, axis, [(0, 1), (1, 0)])


def products_kernel(ring, moved, mine, theirs, *refs):
    parts, refs = refs[:-8], refs[-8:]
    near_in, near_weight, far, wide, strips, weights, total, sems = refs
    chips, _, _, columns = moved.shape
    n_dp, rows = len(parts), near_weight.shape[0]
    half = n_dp // 2
    blocks = far.shape[0]

    arrive = [
        pltpu.make_async_copy(moved.at[:, ring[k]], strips.at[k], sems.at[k]) for k in range(n_dp)
    ]
    for copy in arrive:
        copy.start()
    fetch = []
    for h in range(2):
        cut = pl.ds(h * half * columns, half * columns)
        at = n_dp + 3 * h
        fetch.append([
            pltpu.make_async_copy(moved.at[:, pl.ds(h * half, half)], wide.at[h], sems.at[at]),
            pltpu.make_async_copy(mine.at[:, cut], weights.at[0, h], sems.at[at + 1]),
            pltpu.make_async_copy(theirs.at[:, cut], weights.at[1, h], sems.at[at + 2]),
        ])
        for copy in fetch[h]:
            copy.start()

    for h in range(2):
        for copy in arrive[h * half:(h + 1) * half]:
            copy.wait()
        right = jnp.concatenate(
            [strips[k, i] for k in range(h * half, (h + 1) * half) for i in range(chips)], 0
        )
        left = jnp.concatenate([part[...] for part in parts[h * half:(h + 1) * half]], 1)
        term = jnp.dot(left, right, preferred_element_type=jnp.float32)
        if h == 0:
            total[...] = term
        else:
            near_weight[...] = total[:rows] + term[:rows]
            part = total[rows:] + term[rows:]
            far[:, :, rows:] = part.reshape(blocks, -1, columns).astype(far.dtype)

    sums = [None, None]
    for h in range(2):
        for copy in fetch[h]:
            copy.wait()
        left = jnp.concatenate(
            [jnp.concatenate([wide[h, i, j] for i in range(chips)], 0) for j in range(half)], 1
        )
        for at in range(NC):
            term = lax.dot_general(
                left, weights[at, h], (((1,), (1,)), ((), ())), preferred_element_type=jnp.float32
            )
            sums[at] = term if h == 0 else sums[at] + term
    near_in[...] = sums[0].reshape(blocks, -1, rows).astype(near_in.dtype)
    far[:, :, :rows] = sums[1].reshape(blocks, -1, rows).astype(far.dtype)


def products(ring, moved, weight, weight_other, parts, held):
    chips, _, deep, columns = moved.shape
    n_dp, rows = len(parts), weight.shape[0]
    blocks = chips * deep // held
    vmem, whole = pl.BlockSpec(memory_space=pltpu.VMEM), pl.BlockSpec(memory_space=pl.ANY)
    return pl.pallas_call(
        products_kernel,
        out_shape=(
            jax.ShapeDtypeStruct((blocks, held, rows), jnp.bfloat16),
            jax.ShapeDtypeStruct((rows, columns), jnp.float32),
            jax.ShapeDtypeStruct((blocks, held, rows + columns), jnp.bfloat16),
        ),
        in_specs=[pl.BlockSpec(memory_space=pltpu.SMEM), whole, pl.BlockSpec(memory_space=pltpu.HBM), whole]
        + [vmem] * len(parts),
        out_specs=(vmem, vmem, vmem),
        scratch_shapes=[
            pltpu.VMEM((2, chips, n_dp // 2, deep, columns), jnp.bfloat16),
            pltpu.VMEM((n_dp, chips, deep, columns), jnp.bfloat16),
            pltpu.VMEM((NC, 2, rows, n_dp // 2 * columns), jnp.bfloat16),
            pltpu.VMEM((NC * rows, columns), jnp.float32),
            pltpu.SemaphoreType.DMA((n_dp + 6,)),
        ],
        compiler_params=pltpu.CompilerParams(vmem_limit_bytes=50 * 1024 * 1024),
        cost_estimate=pl.CostEstimate(
            flops=8 * blocks * held * rows * n_dp * columns, bytes_accessed=17 * 1024 * 1024, transcendentals=0
        ),
    )(ring, moved, weight, weight_other, *parts)


def finish_kernel(place, near_in, near_weight, far, grad_in, grad_weight):
    zh, c = place[2], place[3]
    rows = near_in.shape[-1]
    for part, core in ((near_in, c), (far, 1 - c)):
        for at in range(near_in.shape[0]):
            at2, at1, turned = at // (NX * NZ), (at // NZ) % NX, at % NZ
            px, py = jnp.where(core == 0, at1, at2), jnp.where(core == 0, at2, at1)
            z = zh if turned == 0 else 1 - zh
            grad_in[((px * NY + py) * NZ + z) * NC + core] = part[at, :, :rows]
    part = far[:, :, rows:].astype(jnp.float32).reshape(near_weight.shape)
    grad_weight[...] = (near_weight[...] + part).astype(grad_weight.dtype)


def finish(place, near_in, near_weight, far):
    blocks, held, rows = near_in.shape
    vmem = pl.BlockSpec(memory_space=pltpu.VMEM)
    return pl.pallas_call(
        finish_kernel,
        out_shape=(
            jax.ShapeDtypeStruct((NC * blocks, held, rows), jnp.bfloat16),
            jax.ShapeDtypeStruct(near_weight.shape, jnp.bfloat16),
        ),
        in_specs=[pl.BlockSpec(memory_space=pltpu.SMEM), vmem, vmem, vmem],
        out_specs=(vmem, vmem),
        compiler_params=pltpu.CompilerParams(vmem_limit_bytes=8 * 1024 * 1024),
    )(place, near_in, near_weight, far)


def body(attn, grad_out, weight):
    place = jnp.stack([lax.axis_index(a) for a in TENSOR + ("dp",)]).astype(jnp.int32)
    zh, c, dp = place[2], place[3], place[4]
    n_dp = lax.axis_size("dp")
    rows = attn.shape[1]
    held, width = grad_out.shape
    columns = width // n_dp
    blocks = NX * NY * NZ
    tokens = blocks * held
    deep = NZ * held

    parts = attn.reshape(NX, NY, NZ, NC, held, rows)
    low, high = parts[:, :, :, 0].swapaxes(0, 1), parts[:, :, :, 1]
    mine = jnp.where(c == 0, low, high).reshape(tokens, rows).T
    other = jnp.where(c == 0, high, low).reshape(tokens, rows).T
    wide = jnp.concatenate([mine, swap(other, "core")], 0)

    strips = jnp.broadcast_to(
        grad_out.reshape(held, n_dp, 1, columns).transpose(1, 2, 0, 3), (n_dp, NZ, held, columns)
    ).reshape(n_dp * deep, columns)
    sliced = lax.all_to_all(strips, ("dp", "zh"), 0, 0, tiled=True).reshape(n_dp, deep, columns)
    own = lax.broadcasted_iota(jnp.int32, (LAST, 1, 1), 0) == dp
    others = jnp.where(own, sliced[LAST:], sliced[:LAST]).reshape(LAST * deep, columns)
    both = jnp.concatenate([grad_out, swap(grad_out, "zh")], 0)
    both = both.reshape(deep, n_dp, columns).swapaxes(0, 1).reshape(n_dp * deep, columns)

    weight_other = swap(weight, "core")
    wide, both = lax.optimization_barrier((wide, both))
    ahead, back = [wide, turn(wide, 1)], [wide]
    both, ahead[1] = lax.optimization_barrier((both, ahead[1]))
    moved = spread(jnp.concatenate([both, others], 0), True)
    back.append(turn(wide, -1))
    moved, back[1] = lax.optimization_barrier((moved, back[1]))
    moved = spread(moved, False).reshape(NX * NY, n_dp + LAST, deep, columns)
    ahead.append(turn(ahead[-1], 1))
    back.append(turn(back[-1], -1))
    ahead[2], back[2] = lax.optimization_barrier((ahead[2], back[2]))
    for _ in range(n_dp // 2 - 2):
        ahead.append(turn(ahead[-1], 1))
    for _ in range(n_dp // 2 - 3):
        back.append(turn(back[-1], -1))
    ring = lax.dynamic_slice_in_dim(jnp.asarray(BEFORE, jnp.int32), dp * n_dp, n_dp)

    first = wide.reshape(NC * rows, NX * NY, NZ, held)
    first = jnp.where(zh == 0, first, first[:, :, ::-1]).reshape(NC * rows, tokens)
    near_in, near_weight, far = products(ring, moved, weight, weight_other, [first] + ahead[1:] + back[:0:-1], held)
    far = swap(far, "core")
    grad_in, grad_weight = finish(place, near_in, near_weight, far)
    return grad_in.reshape(NC * tokens, rows), grad_weight


def solution(mesh):
    n_dp = mesh.shape["dp"]
    fine = Mesh(mesh.devices.reshape(n_dp, NX, NY, NZ, NC), AXES)
    in_specs = (P("dp", TENSOR), P(("dp",) + TENSOR, None), P(TENSOR, None))
    out_specs = (P("dp", TENSOR), P(TENSOR, "dp"))
    return jax.shard_map(body, mesh=fine, in_specs=in_specs, out_specs=out_specs, check_vma=False)
```

```python
import functools

import jax
import jax.numpy as jnp
from jax import lax
from jax.experimental import pallas as pl
from jax.experimental.pallas import tpu as pltpu
from jax.sharding import Mesh, PartitionSpec as P

NX, NY, NZ, NC = 4, 4, 2, 2
AXES = ("dp", "x", "y", "zh", "core")
RING = (0, 2, 4, 6, 7, 5, 3, 1)
LAST = len(RING) - 1


def place_of(g, other):
    return g if other == g else len(RING) + (g if other == LAST else other)


BEFORE = tuple(
    place_of(g, RING[(RING.index(g) - k) % len(RING)]) for g in range(len(RING)) for k in range(len(RING))
)
TENSOR = ("x", "y", "zh", "core")


def lines(first):
    def at(x, y, z, c):
        return ((x * NY + y) * NZ + z) * NC + c

    groups = []
    for z in range(NZ):
        for c in range(NC):
            for k in range(NX):
                if (c == 0) == first:
                    groups.append([at(i, k, z, c) for i in range(NX)])
                else:
                    groups.append([at(k, i, z, c) for i in range(NY)])
    return groups


def spread(values, first, before=None):
    n = values.shape[0]
    copies = jnp.broadcast_to(values[None], (NX,) + values.shape).reshape((NX * n,) + values.shape[1:])
    if before is not None:
        copies, _ = lax.optimization_barrier((copies, before))
    return lax.all_to_all(copies, TENSOR, 0, 0, axis_index_groups=lines(first), tiled=True)


def turn(values, step):
    pairs = [(RING[i], RING[(i + step) % len(RING)]) for i in range(len(RING))]
    return lax.ppermute(values, "dp", pairs)


def swap(values, axis):
    return lax.ppermute(values, axis, [(0, 1), (1, 0)])


def products_kernel(ring, moved, mine, theirs, *refs):
    parts, refs = refs[:-8], refs[-8:]
    near_in, near_weight, far, wide, strips, weights, total, sems = refs
    chips, _, _, columns = moved.shape
    n_dp, rows = len(parts), near_weight.shape[0]
    half = n_dp // 2
    blocks = far.shape[0]

    arrive = [
        pltpu.make_async_copy(moved.at[:, ring[k]], strips.at[k], sems.at[k]) for k in range(n_dp)
    ]
    for copy in arrive:
        copy.start()
    fetch = []
    for h in range(2):
        cut = pl.ds(h * half * columns, half * columns)
        at = n_dp + 3 * h
        fetch.append([
            pltpu.make_async_copy(moved.at[:, pl.ds(h * half, half)], wide.at[h], sems.at[at]),
            pltpu.make_async_copy(mine.at[:, cut], weights.at[0, h], sems.at[at + 1]),
            pltpu.make_async_copy(theirs.at[:, cut], weights.at[1, h], sems.at[at + 2]),
        ])
        for copy in fetch[h]:
            copy.start()

    for h in range(2):
        for copy in arrive[h * half:(h + 1) * half]:
            copy.wait()
        right = jnp.concatenate(
            [strips[k, i] for k in range(h * half, (h + 1) * half) for i in range(chips)], 0
        )
        left = jnp.concatenate([part[...] for part in parts[h * half:(h + 1) * half]], 1)
        term = jnp.dot(left, right, preferred_element_type=jnp.float32)
        if h == 0:
            total[...] = term
        else:
            near_weight[...] = total[:rows] + term[:rows]
            part = total[rows:] + term[rows:]
            far[:, :, rows:] = part.reshape(blocks, -1, columns).astype(far.dtype)

    sums = [None, None]
    for h in range(2):
        for copy in fetch[h]:
            copy.wait()
        left = jnp.concatenate(
            [jnp.concatenate([wide[h, i, j] for i in range(chips)], 0) for j in range(half)], 1
        )
        for at in range(NC):
            term = lax.dot_general(
                left, weights[at, h], (((1,), (1,)), ((), ())), preferred_element_type=jnp.float32
            )
            sums[at] = term if h == 0 else sums[at] + term
    near_in[...] = sums[0].reshape(blocks, -1, rows).astype(near_in.dtype)
    far[:, :, :rows] = sums[1].reshape(blocks, -1, rows).astype(far.dtype)


def products(ring, moved, weight, weight_other, parts, held):
    chips, _, deep, columns = moved.shape
    n_dp, rows = len(parts), weight.shape[0]
    blocks = chips * deep // held
    vmem, whole = pl.BlockSpec(memory_space=pltpu.VMEM), pl.BlockSpec(memory_space=pl.ANY)
    return pl.pallas_call(
        products_kernel,
        out_shape=(
            jax.ShapeDtypeStruct((blocks, held, rows), jnp.bfloat16),
            jax.ShapeDtypeStruct((rows, columns), jnp.float32),
            jax.ShapeDtypeStruct((blocks, held, rows + columns), jnp.bfloat16),
        ),
        in_specs=[pl.BlockSpec(memory_space=pltpu.SMEM), whole, pl.BlockSpec(memory_space=pltpu.HBM), whole]
        + [vmem] * len(parts),
        out_specs=(vmem, vmem, vmem),
        scratch_shapes=[
            pltpu.VMEM((2, chips, n_dp // 2, deep, columns), jnp.bfloat16),
            pltpu.VMEM((n_dp, chips, deep, columns), jnp.bfloat16),
            pltpu.VMEM((NC, 2, rows, n_dp // 2 * columns), jnp.bfloat16),
            pltpu.VMEM((NC * rows, columns), jnp.float32),
            pltpu.SemaphoreType.DMA((n_dp + 6,)),
        ],
        compiler_params=pltpu.CompilerParams(vmem_limit_bytes=50 * 1024 * 1024),
        cost_estimate=pl.CostEstimate(
            flops=8 * blocks * held * rows * n_dp * columns, bytes_accessed=17 * 1024 * 1024, transcendentals=0
        ),
    )(ring, moved, weight, weight_other, *parts)


def finish_kernel(place, near_in, near_weight, far, grad_in, grad_weight):
    zh, c = place[2], place[3]
    rows = near_in.shape[-1]
    for part, core in ((near_in, c), (far, 1 - c)):
        for at in range(near_in.shape[0]):
            at2, at1, turned = at // (NX * NZ), (at // NZ) % NX, at % NZ
            px, py = jnp.where(core == 0, at1, at2), jnp.where(core == 0, at2, at1)
            z = zh if turned == 0 else 1 - zh
            grad_in[((px * NY + py) * NZ + z) * NC + core] = part[at, :, :rows]
    part = far[:, :, rows:].astype(jnp.float32).reshape(near_weight.shape)
    grad_weight[...] = (near_weight[...] + part).astype(grad_weight.dtype)


def finish(place, near_in, near_weight, far):
    blocks, held, rows = near_in.shape
    vmem = pl.BlockSpec(memory_space=pltpu.VMEM)
    return pl.pallas_call(
        finish_kernel,
        out_shape=(
            jax.ShapeDtypeStruct((NC * blocks, held, rows), jnp.bfloat16),
            jax.ShapeDtypeStruct(near_weight.shape, jnp.bfloat16),
        ),
        in_specs=[pl.BlockSpec(memory_space=pltpu.SMEM), vmem, vmem, vmem],
        out_specs=(vmem, vmem),
        compiler_params=pltpu.CompilerParams(vmem_limit_bytes=8 * 1024 * 1024),
    )(place, near_in, near_weight, far)


def body(attn, grad_out, weight):
    place = jnp.stack([lax.axis_index(a) for a in TENSOR + ("dp",)]).astype(jnp.int32)
    zh, c, dp = place[2], place[3], place[4]
    n_dp = lax.axis_size("dp")
    rows = attn.shape[1]
    held, width = grad_out.shape
    columns = width // n_dp
    blocks = NX * NY * NZ
    tokens = blocks * held
    deep = NZ * held

    parts = attn.reshape(NX, NY, NZ, NC, held, rows)
    low, high = parts[:, :, :, 0].swapaxes(0, 1), parts[:, :, :, 1]
    mine = jnp.where(c == 0, low, high).reshape(tokens, rows).T
    other = jnp.where(c == 0, high, low).reshape(tokens, rows).T
    wide = jnp.concatenate([mine, swap(other, "core")], 0)

    strips = jnp.broadcast_to(
        grad_out.reshape(held, n_dp, 1, columns).transpose(1, 2, 0, 3), (n_dp, NZ, held, columns)
    ).reshape(n_dp * deep, columns)
    sliced = lax.all_to_all(strips, ("dp", "zh"), 0, 0, tiled=True).reshape(n_dp, deep, columns)
    own = lax.broadcasted_iota(jnp.int32, (LAST, 1, 1), 0) == dp
    others = jnp.where(own, sliced[LAST:], sliced[:LAST]).reshape(LAST * deep, columns)
    both = jnp.concatenate([grad_out, swap(grad_out, "zh")], 0)
    both = both.reshape(deep, n_dp, columns).swapaxes(0, 1).reshape(n_dp * deep, columns)

    weight_other = swap(weight, "core")
    wide, both = lax.optimization_barrier((wide, both))
    ahead, back = [wide, turn(wide, 1)], [wide]
    moved = spread(jnp.concatenate([both, others], 0), True, ahead[1])
    back.append(turn(wide, -1))
    moved, back[1] = lax.optimization_barrier((moved, back[1]))
    moved = spread(moved, False).reshape(NX * NY, n_dp + LAST, deep, columns)
    ahead.append(turn(ahead[-1], 1))
    back.append(turn(back[-1], -1))
    ahead[2], back[2] = lax.optimization_barrier((ahead[2], back[2]))
    for _ in range(n_dp // 2 - 2):
        ahead.append(turn(ahead[-1], 1))
    for _ in range(n_dp // 2 - 3):
        back.append(turn(back[-1], -1))
    ring = lax.dynamic_slice_in_dim(jnp.asarray(BEFORE, jnp.int32), dp * n_dp, n_dp)

    first = wide.reshape(NC * rows, NX * NY, NZ, held)
    first = jnp.where(zh == 0, first, first[:, :, ::-1]).reshape(NC * rows, tokens)
    near_in, near_weight, far = products(ring, moved, weight, weight_other, [first] + ahead[1:] + back[:0:-1], held)
    far = swap(far, "core")
    grad_in, grad_weight = finish(place, near_in, near_weight, far)
    return grad_in.reshape(NC * tokens, rows), grad_weight


def solution(mesh):
    n_dp = mesh.shape["dp"]
    fine = Mesh(mesh.devices.reshape(n_dp, NX, NY, NZ, NC), AXES)
    in_specs = (P("dp", TENSOR), P(("dp",) + TENSOR, None), P(TENSOR, None))
    out_specs = (P("dp", TENSOR), P(TENSOR, "dp"))
    return jax.shard_map(body, mesh=fine, in_specs=in_specs, out_specs=out_specs, check_vma=False)
```
